1024 devices in a mesh: section: 16 (over x, y_lo, core), expert: 64 (over y_hi, z).
Axes of the slice: x: 4, y: 4 (y_hi: 2, y_lo: 2; y = y_hi * 2 + y_lo), z: 32, core: 2. Of those that a mesh axis runs over, the one named last changes fastest.
Arguments:
- grad_rows: bfloat16 [16, 2, 8192, 1024], P('section', None, 'expert'), may hold values from -1 to 1
- owner_ids: int32 [16, 2, 8192, 1], P('section', None, 'expert'), may hold values from 0 to 63; in each aligned block of 128 rows (0 to 127, 128 to 255, ..., all dimensions but the last counted through in order) at most 4 rows name the same one
- saved_hidden: bfloat16 [16, 2, 64, 256, 384], P('section', None, 'expert'), may hold values from -6 to 6
- momentum: bfloat16 [16, 64, 384, 1024], P('section', 'expert'), may hold values from -32 to 32
Outputs:
- new_momentum: bfloat16 [16, 64, 384, 1024], P('section', 'expert')
- update_step: bfloat16 [16, 64, 384, 1024], P('section', 'expert')
The draws below stay inside these ranges and needn't reach their ends.
Inputs may be any that keep to these rules, and one draw needn't show every extreme that they name: `owner_ids`: within each aligned block of 128 rows of one section and direction, no owner is named by more than 4 rows, a bound that some block reaches.
All inputs are finite; a program needn't handle non-finite values.
Results may differ from the reference program's by a relative error of at most 0.0065.
Values may be sent and summed in bfloat16 or wider, within the bound.
A program may use at most 32 MiB of HBM per device.

```python
import math
import jax
import jax.numpy as jnp
import numpy as np
from jax import lax

D = 1024
FF = 384
ROWS_DEV = 128
ITERS = 2
SECTIONS = 16
EXPERTS = 64
CAP = 4
SLOTS = 256
ROWS = 8192


def draw_momentum(key, part):
    key_rows = jax.random.fold_in(key, 11)
    key_cols = jax.random.fold_in(key, 12)
    key_base = jax.random.fold_in(key, 13)
    row_scale = jnp.exp(jax.random.uniform(key_rows, (SECTIONS, EXPERTS, FF, 1), jnp.float32, 0.0, 1.1513))
    col_scale = jnp.exp(jax.random.uniform(key_cols, (SECTIONS, EXPERTS, 1, D), jnp.float32, 0.0, 1.1513))
    values = jax.random.normal(key_base, (SECTIONS, EXPERTS, FF, D), jnp.float32)
    return jnp.clip(0.5 * row_scale * col_scale * values, -32.0, 32.0).astype(jnp.bfloat16)


def steps_of(key, dims, shards, smallest, high):
    def one(dim, parts):
        draws = jax.random.uniform(jax.random.fold_in(jax.random.fold_in(key, 6), dim), (parts,), jnp.float32, smallest / len(shards), high / len(shards))
        return jnp.repeat(jnp.exp(draws), dims[dim] // parts).reshape((-1,) + (1,) * (len(dims) - dim - 1))

    level = one(*shards[0])
    for cut in shards[1:]:
        level = level * one(*cut)
    return level


def routed_block(own_key, own, number, rows, count, top, bound, lean):
    ranking = jax.random.permutation(own_key, count)
    crowded, common = load_shares(count, rows * top, bound, lean, True), load_shares(count, rows * top, bound, lean, False)
    places = jnp.arange(count)

    def named(sizes, offset_by):
        used = int((sizes > 0).sum())
        fixed = max(1, used // 4)
        moved = fixed + (places - fixed + offset_by * (used - fixed)) % max(1, count - fixed)
        return jnp.zeros((count,), jnp.int32).at[ranking[jnp.where(places < fixed, places, moved)]].set(jnp.asarray(sizes, jnp.int32))

    sizes = jnp.where(number % 4 == 0, named(crowded, number // 4), named(common, number - number // 4 - 1))
    mixed = jax.random.permutation(jax.random.fold_in(own, 3), count)
    source_of, taker = mixed[0:count // 2 * 2:2], mixed[1:count // 2 * 2:2]
    room = jnp.minimum(sizes[source_of] - 1, bound - sizes[taker]) // 2
    room = jnp.where((source_of == ranking[0]) | (taker == ranking[0]) | (sizes[taker] == 0), 0, jnp.maximum(room, 0))
    moved = jax.random.randint(jax.random.fold_in(own, 4), (count // 2,), 0, 1 << 20) % (room + 1)
    sizes = sizes.at[source_of].add(-moved).at[taker].add(moved)
    labels = jnp.searchsorted(jnp.cumsum(sizes), jnp.arange(rows * top), side="right").astype(jnp.int32)
    grid = labels.reshape(top, rows).T
    grid = grid[jax.random.permutation(jax.random.fold_in(own, 1), rows)]
    offset_by = jax.random.randint(jax.random.fold_in(own, 2), (rows, 1), 0, top)
    return jnp.take_along_axis(grid, (jnp.arange(top)[None, :] + offset_by) % top, axis=1)


def load_shares(count, total, most, lean, full):
    loads = [(1 << 20) // math.isqrt(standing ** lean) + 1 for standing in range(1, count + 1)]
    largest = most if full else min(most, max(-(-total // count), total * loads[0] // sum(loads)))
    least = 1 if total - largest >= count - 1 else 0
    holding, spare = [largest] + [least] * (count - 1), total - largest - least * (count - 1)
    while spare > 0:
        candidates = [i for i in range(1, count) if holding[i] < largest] or [i for i in range(1, count) if holding[i] < most]
        whole, left = sum([loads[i] for i in candidates]), spare
        for i in candidates:
            addition = min(most - holding[i], max(1, left * loads[i] // whole), spare)
            holding[i] = holding[i] + addition
            spare = spare - addition
    return np.array(holding)


def bell_draw(rng, extent, deviation, reach, pieces=(), kind=jnp.bfloat16):
    result = jax.random.normal(rng, extent, jnp.float32) * deviation
    if len(pieces) > 0:
        result = steps_of(rng, extent, pieces, -0.22, 0.18) * result
    return jnp.clip(result, min=-reach, max=reach).astype(kind)


def setup_inputs(seed: int = 0) -> dict:
    seeds = jax.random.split(jax.random.key(seed), 5)
    grad_rows = bell_draw(seeds[0], (SECTIONS, 2, ROWS, D), 0.125, 1.0, ((0, 16), (2, 64)))
    owner_ids_keys = jax.random.split(jax.random.fold_in(seeds[1], 1), SECTIONS * 2 * ROWS // ROWS_DEV)
    owner_ids_turns = jax.random.permutation(jax.random.fold_in(seeds[1], 3), SECTIONS * 2 * ROWS // ROWS_DEV)
    owner_ids = jax.vmap(lambda own, number: routed_block(jax.random.fold_in(seeds[1], 2), own, number, ROWS_DEV, EXPERTS, 1, CAP, 2))(owner_ids_keys, owner_ids_turns).reshape((SECTIONS, 2, ROWS, 1))
    saved_hidden = bell_draw(seeds[2], (SECTIONS, 2, EXPERTS, SLOTS, FF), 1.0, 6.0, ((0, 16), (2, 64)))
    momentum = draw_momentum(jax.random.fold_in(seeds[4], 71), 0)
    return dict(grad_rows=grad_rows, owner_ids=owner_ids, saved_hidden=saved_hidden, momentum=momentum)


momentum_decay = 0.95
coef_first = 3.4445
coef_second = -4.775
coef_third = 2.0315
norm_epsilon = 1e-06

def slot_rows(row_block, owners):
    owner_grid = owners.reshape(EXPERTS, ROWS_DEV).astype(jnp.int32)
    onehot = (owner_grid[:, :, None] == jnp.arange(EXPERTS, dtype=jnp.int32)[None, None, :]).astype(jnp.int32)
    before = jnp.cumsum(onehot, axis=1) - onehot
    within = lax.optimization_barrier(jnp.sum(before * onehot, axis=2))
    source_index = jnp.arange(EXPERTS, dtype=jnp.int32)[:, None]
    target = owner_grid * SLOTS + source_index * CAP + within
    placed = jnp.zeros((EXPERTS * SLOTS, D), jnp.bfloat16).at[target.reshape(-1)].set(row_block)
    return placed.reshape(EXPERTS, SLOTS, D)

def contract(hidden_block, grad_block):
    product = lax.dot_general(hidden_block, grad_block, (((0,), (0,)), ((), ())), preferred_element_type=jnp.float32)
    return product.astype(jnp.bfloat16)

def orthogonalize(accum):
    norm_scale = jnp.sqrt(jnp.sum(accum * accum)) + norm_epsilon
    current = (accum / norm_scale).astype(jnp.bfloat16)
    for iteration in range(ITERS):
        gram_matrix = jnp.dot(current, current.T, preferred_element_type=jnp.float32).astype(jnp.bfloat16)
        once_applied = jnp.dot(gram_matrix, current, preferred_element_type=jnp.float32).astype(jnp.bfloat16)
        twice_applied = jnp.dot(gram_matrix, once_applied, preferred_element_type=jnp.float32).astype(jnp.bfloat16)
        combined = coef_first * current.astype(jnp.float32) + coef_second * once_applied.astype(jnp.float32) + coef_third * twice_applied.astype(jnp.float32)
        if iteration == ITERS - 1:
            combined = combined * math.sqrt(D)
        current = combined.astype(jnp.bfloat16)
    return current

def reference(grad_rows, owner_ids, saved_hidden, momentum):

    def one_layer(layer_index):
        mirror = SECTIONS - 1 - layer_index
        front_slots = slot_rows(grad_rows[layer_index, 0], owner_ids[layer_index, 0, :, 0])
        back_slots = slot_rows(grad_rows[mirror, 1], owner_ids[mirror, 1, :, 0])

        def one_expert(expert_index):
            near_part = contract(saved_hidden[layer_index, 0, expert_index], front_slots[expert_index])
            far_part = contract(saved_hidden[mirror, 1, expert_index], back_slots[expert_index])
            accum = momentum_decay * momentum[layer_index, expert_index].astype(jnp.float32) + near_part.astype(jnp.float32) + far_part.astype(jnp.float32)
            return (accum.astype(jnp.bfloat16), orthogonalize(accum))
        return lax.map(one_expert, jnp.arange(EXPERTS, dtype=jnp.int32))
    new_momentum, update_step = lax.map(one_layer, jnp.arange(SECTIONS, dtype=jnp.int32))
    return (new_momentum, update_step)
```

```python
import functools
import math

import jax
import jax.numpy as jnp
from jax import lax
from jax.experimental import pallas as pl
from jax.experimental.pallas import tpu as pltpu
from jax.sharding import PartitionSpec as P

MESH = pl.DeviceIdType.MESH
ITERS = 2
ROUND_Z = 32

momentum_decay = 0.95
coef_first = 3.4445
coef_second = -4.775
coef_third = 2.0315
norm_epsilon = 1e-06

f32 = jnp.float32
bf16 = jnp.bfloat16


def nn(a, b):
    return lax.dot_general(a, b, (((1,), (0,)), ((), ())), preferred_element_type=f32)


def nt(a, b):
    return lax.dot_general(a, b, (((1,), (1,)), ((), ())), preferred_element_type=f32)


def tn(a, b):
    return lax.dot_general(a, b, (((0,), (0,)), ((), ())), preferred_element_type=f32)


def kernel(
    sections, peers, cap, parts,
    grad_hbm, owner_ref, hidden_hbm, mom_hbm, newm_hbm, upd_hbm,
    grad, hidden, mom, send, recv, spread, far_out, far_in, accum, x, gram, once, newm, upd,
    in_sems, own_sems, send_sems, recv_sems, mir_send, mir_recv, out_sems,
):
    rows = grad.shape[1]
    width = grad.shape[2]
    unit = cap * parts
    chunk = width // parts
    total = peers * unit
    sec = lax.axis_index("section")
    me = lax.axis_index("expert")
    mirror = sections - 1 - sec
    half = peers // 2
    side, spot = me // half, lax.rem(me, half)

    loads = [
        pltpu.make_async_copy(grad_hbm.at[1], grad.at[1], in_sems.at[0]),
        pltpu.make_async_copy(grad_hbm.at[0], grad.at[0], in_sems.at[1]),
        pltpu.make_async_copy(hidden_hbm, hidden, in_sems.at[2]),
        pltpu.make_async_copy(mom_hbm, mom, in_sems.at[3]),
    ]
    for load in loads:
        load.start()

    barrier = pltpu.get_barrier_semaphore()

    def greet(step, carry):
        peer = lax.rem(me + step, peers)
        pl.semaphore_signal(barrier, inc=1, device_id=(sec, peer), device_id_type=MESH)
        return carry

    lax.fori_loop(1, peers, greet, 0)
    pl.semaphore_signal(barrier, inc=1, device_id=(mirror, me), device_id_type=MESH)

    def pack(direction):
        owners = owner_ref[direction]
        hot = (lax.broadcasted_iota(jnp.int32, (peers, rows), 0) == owners).astype(bf16)
        earlier = (
            lax.broadcasted_iota(jnp.int32, (rows, rows), 0)
            < lax.broadcasted_iota(jnp.int32, (rows, rows), 1)
        ).astype(bf16)
        before = nn(hot, earlier)
        within = jnp.sum(before * hot.astype(f32), axis=0, keepdims=True).astype(jnp.int32)
        target = owners * unit + within
        line = lax.broadcasted_iota(jnp.int32, (total, rows), 0)
        packed = None
        for part in range(parts):
            pick = (line == target + part * cap).astype(bf16)
            term = nn(pick, grad[direction, :, part * chunk : (part + 1) * chunk])
            packed = term if packed is None else packed + term
        send[direction] = packed.astype(bf16)

    def copy_to(direction, peer):
        return pltpu.make_async_remote_copy(
            src_ref=send.at[direction, pl.ds(pl.multiple_of(peer * unit, unit), unit)],
            dst_ref=recv.at[direction, pl.ds(pl.multiple_of(me * unit, unit), unit)],
            send_sem=send_sems.at[direction],
            recv_sem=recv_sems.at[direction],
            device_id=(sec, peer),
            device_id_type=MESH,
        )

    def own_copy(direction):
        mine = pl.ds(pl.multiple_of(me * unit, unit), unit)
        return pltpu.make_async_copy(
            send.at[direction, mine], recv.at[direction, mine], own_sems.at[direction]
        )

    def send_all(direction):
        def step(t, carry):
            length = half // 2 - (t + 1) // 2
            shift = lax.rem(t, 2) * 2 * length - length
            place = lax.rem(spot + shift + half, half)
            copy_to(direction, side * half + place).start()
            copy_to(direction, (1 - side) * half + place).start()
            return carry

        lax.fori_loop(0, half - 1, step, 0)
        copy_to(direction, (1 - side) * half + spot).start()
        own_copy(direction).start()

    def all_but_one(direction):
        most = pl.ds(0, (peers - 1) * unit)
        return pltpu.make_async_remote_copy(
            src_ref=send.at[direction, most],
            dst_ref=recv.at[direction, most],
            send_sem=send_sems.at[direction],
            recv_sem=recv_sems.at[direction],
            device_id=(sec, me),
            device_id_type=MESH,
        )

    loads[0].wait()
    pack(1)
    pl.semaphore_wait(barrier, peers)
    send_all(1)
    loads[1].wait()
    pack(0)
    send_all(0)

    loads[2].wait()
    slots = peers * cap
    line = lax.broadcasted_iota(jnp.int32, (slots, total), 1)
    slot = lax.broadcasted_iota(jnp.int32, (slots, total), 0)
    expand = (line // unit * cap + lax.rem(line, cap) == slot).astype(bf16)
    for direction in (1, 0):
        wide = tn(hidden[direction], expand).astype(bf16)
        which = lax.rem(lax.broadcasted_iota(jnp.int32, wide.shape, 1) // cap, parts)
        for part in range(parts):
            spread[direction, part] = jnp.where(which == part, wide, jnp.zeros_like(wide))

    loads[3].wait()

    own_copy(1).wait()
    all_but_one(1).wait_recv()
    for part in range(parts):
        at = slice(part * chunk, (part + 1) * chunk)
        far_out[:, at] = nn(spread[1, part], recv[1]).astype(bf16)
    exchange = pltpu.make_async_remote_copy(
        src_ref=far_out,
        dst_ref=far_in,
        send_sem=mir_send,
        recv_sem=mir_recv,
        device_id=(mirror, me),
        device_id_type=MESH,
    )
    exchange.start()

    exchange.wait_recv()
    for part in range(parts):
        at = slice(part * chunk, (part + 1) * chunk)
        accum[:, at] = mom[:, at].astype(f32) * momentum_decay

    own_copy(0).wait()
    all_but_one(0).wait_recv()
    squares = None
    for part in range(parts):
        at = slice(part * chunk, (part + 1) * chunk)
        near = nn(spread[0, part], recv[0]).astype(bf16)
        value = accum[:, at] + near.astype(f32) + far_in[:, at].astype(f32)
        accum[:, at] = value
        newm[:, at] = value.astype(bf16)
        square = jnp.sum(value * value, axis=0, keepdims=True)
        square = jnp.sum(square, axis=1, keepdims=True)
        squares = square if squares is None else squares + square
    save_newm = pltpu.make_async_copy(newm, newm_hbm, out_sems.at[0])
    save_newm.start()

    scale = 1.0 / (jnp.sqrt(squares) + norm_epsilon)
    for part in range(parts):
        at = slice(part * chunk, (part + 1) * chunk)
        x[:, at] = (accum[:, at] * scale).astype(bf16)

    saves = []
    for iteration in range(ITERS):
        gram[...] = nt(x[...], x[...]).astype(bf16)
        for part in range(parts):
            at = slice(part * chunk, (part + 1) * chunk)
            current = x[:, at]
            first = nn(gram[...], current).astype(bf16)
            second = nn(gram[...], first).astype(bf16)
            combined = (
                coef_first * current.astype(f32)
                + coef_second * first.astype(f32)
                + coef_third * second.astype(f32)
            )
            if iteration == ITERS - 1:
                upd[:, at] = (combined * math.sqrt(width)).astype(bf16)
            else:
                x[:, at] = combined.astype(bf16)
    save_upd = pltpu.make_async_copy(upd, upd_hbm, out_sems.at[1])
    save_upd.start()

    all_but_one(1).wait_send()
    all_but_one(0).wait_send()
    exchange.wait_send()
    save_newm.wait()
    save_upd.wait()


def solution(mesh):
    sections, peers = mesh.shape["section"], mesh.shape["expert"]

    def per_device(grad_rows, owner_ids, saved_hidden, momentum):
        _, _, rows, width = grad_rows.shape
        slots, ff = saved_hidden.shape[3:]
        cap = slots // peers
        parts = 16 // cap
        total = slots * parts
        chunk = width // parts
        hbm = pl.BlockSpec(memory_space=pl.ANY)
        vmem = pl.BlockSpec(memory_space=pltpu.VMEM)
        newm, upd = pl.pallas_call(
            functools.partial(kernel, sections, peers, cap, parts),
            out_shape=[jax.ShapeDtypeStruct((ff, width), bf16)] * 2,
            in_specs=[hbm, vmem, hbm, hbm],
            out_specs=[hbm, hbm],
            scratch_shapes=[
                pltpu.VMEM((2, rows, width), bf16),
                pltpu.VMEM((2, slots, ff), bf16),
                pltpu.VMEM((ff, width), bf16),
                pltpu.VMEM((2, total, chunk), bf16),
                pltpu.VMEM((2, total, chunk), bf16),
                pltpu.VMEM((2, parts, ff, total), bf16),
                pltpu.VMEM((ff, width), bf16),
                pltpu.VMEM((ff, width), bf16),
                pltpu.VMEM((ff, width), f32),
                pltpu.VMEM((ff, width), bf16),
                pltpu.VMEM((ff, ff), bf16),
                pltpu.VMEM((ff, width), bf16),
                pltpu.VMEM((ff, width), bf16),
                pltpu.VMEM((ff, width), bf16),
                pltpu.SemaphoreType.DMA((4,)),
                pltpu.SemaphoreType.DMA((2,)),
                pltpu.SemaphoreType.DMA((2,)),
                pltpu.SemaphoreType.DMA((2,)),
                pltpu.SemaphoreType.DMA,
                pltpu.SemaphoreType.DMA,
                pltpu.SemaphoreType.DMA((2,)),
            ],
            compiler_params=pltpu.CompilerParams(
                collective_id=0, has_side_effects=True, vmem_limit_bytes=48 * 2**20
            ),
            name="routed_muon",
        )(
            grad_rows[0],
            owner_ids.reshape(2, 1, rows),
            saved_hidden.reshape(2, slots, ff),
            momentum[0, 0],
        )
        return newm[None, None], upd[None, None]

    placed = (
        P("section", None, "expert", None),
        P("section", None, "expert", None),
        P("section", None, "expert", None, None),
        P("section", "expert", None, None),
    )
    return jax.shard_map(
        per_device,
        mesh=mesh,
        in_specs=placed,
        out_specs=(P("section", "expert", None, None), P("section", "expert", None, None)),
        check_vma=False,
    )
```

```python
import functools
import math

import jax
import jax.numpy as jnp
from jax import lax
from jax.experimental import pallas as pl
from jax.experimental.pallas import tpu as pltpu
from jax.sharding import PartitionSpec as P

MESH = pl.DeviceIdType.MESH
ITERS = 2
LATE = 11
NEAR = 7
VMEM_LIMIT = 60 * 2**20

momentum_decay = 0.95
coef_first = 3.4445
coef_second = -4.775
coef_third = 2.0315
norm_epsilon = 1e-06

f32 = jnp.float32
bf16 = jnp.bfloat16


def nn(a, b):
    return lax.dot_general(a, b, (((1,), (0,)), ((), ())), preferred_element_type=f32)


def nt(a, b):
    return lax.dot_general(a, b, (((1,), (1,)), ((), ())), preferred_element_type=f32)


def tn(a, b):
    return lax.dot_general(a, b, (((0,), (0,)), ((), ())), preferred_element_type=f32)


def exchange_rows(
    sections, peers, cap, parts,
    grad_hbm, owner_hbm, hidden_hbm, mom_hbm, accum_hbm,
    grad, owner_ref, hidden, mom, send, recv, spread, far_out, far_in, accum,
    in_sems, own_sems, send_sems, recv_sems, mir_send, mir_recv, out_sems,
):
    rows = grad.shape[1]
    width = grad.shape[2]
    unit = cap * parts
    chunk = width // parts
    total = peers * unit
    sec = lax.axis_index("section")
    me = lax.axis_index("expert")
    mirror = sections - 1 - sec
    half = peers // 2
    side, spot = me // half, lax.rem(me, half)

    names = pltpu.make_async_copy(owner_hbm, owner_ref, in_sems.at[4])
    names.start()
    loads = [
        pltpu.make_async_copy(grad_hbm.at[1], grad.at[1], in_sems.at[0]),
        pltpu.make_async_copy(grad_hbm.at[0], grad.at[0], in_sems.at[1]),
        pltpu.make_async_copy(hidden_hbm, hidden, in_sems.at[2]),
        pltpu.make_async_copy(mom_hbm, mom, in_sems.at[3]),
    ]
    for load in loads:
        load.start()

    barrier = pltpu.get_barrier_semaphore()

    def greet(step, carry):
        peer = lax.rem(me + step, peers)
        pl.semaphore_signal(barrier, inc=1, device_id=(sec, peer), device_id_type=MESH)
        return carry

    lax.fori_loop(1, peers, greet, 0)
    pl.semaphore_signal(barrier, inc=1, device_id=(mirror, me), device_id_type=MESH)

    def pack(direction):
        owners = owner_ref[direction]
        hot = (lax.broadcasted_iota(jnp.int32, (peers, rows), 0) == owners).astype(bf16)
        earlier = (
            lax.broadcasted_iota(jnp.int32, (rows, rows), 0)
            < lax.broadcasted_iota(jnp.int32, (rows, rows), 1)
        ).astype(bf16)
        before = nn(hot, earlier)
        within = jnp.sum(before * hot.astype(f32), axis=0, keepdims=True).astype(jnp.int32)
        target = owners * unit + within
        line = lax.broadcasted_iota(jnp.int32, (total, rows), 0)
        packed = None
        for part in range(parts):
            pick = (line == target + part * cap).astype(bf16)
            term = nn(pick, grad[direction, :, part * chunk : (part + 1) * chunk])
            packed = term if packed is None else packed + term
        send[direction] = packed.astype(bf16)

    def copy_to(direction, peer):
        return pltpu.make_async_remote_copy(
            src_ref=send.at[direction, pl.ds(pl.multiple_of(peer * unit, unit), unit)],
            dst_ref=recv.at[direction, pl.ds(pl.multiple_of(me * unit, unit), unit)],
            send_sem=send_sems.at[direction],
            recv_sem=recv_sems.at[direction],
            device_id=(sec, peer),
            device_id_type=MESH,
        )

    def own_copy(direction):
        mine = pl.ds(pl.multiple_of(me * unit, unit), unit)
        return pltpu.make_async_copy(
            send.at[direction, mine], recv.at[direction, mine], own_sems.at[direction]
        )

    def send_all(direction):
        def plain(t, carry):
            length = half // 2 - (t + 1) // 2
            shift = lax.rem(t, 2) * 2 * length - length
            place = lax.rem(spot + shift + half, half)
            copy_to(direction, side * half + place).start()
            copy_to(direction, (1 - side) * half + place).start()
            return carry

        def step(last, t, carry):
            length = half // 2 - (t + 1) // 2
            shift = lax.rem(t, 2) * 2 * length - length
            reach = spot + shift
            place = lax.rem(reach + half, half)
            wraps = (reach < 0) | (reach >= half)
            held = (spot >= LATE) & (place >= LATE) & (wraps | (length <= NEAR))

            @pl.when(held if last else jnp.logical_not(held))
            def _():
                copy_to(direction, side * half + place).start()
                copy_to(direction, (1 - side) * half + place).start()

            return carry

        if direction:
            lax.fori_loop(0, half - 1, plain, 0)
        else:
            lax.fori_loop(0, half - 1, functools.partial(step, False), 0)
            lax.fori_loop(0, half - 1, functools.partial(step, True), 0)
        copy_to(direction, (1 - side) * half + spot).start()
        own_copy(direction).start()

    def all_but_one(direction):
        most = pl.ds(0, (peers - 1) * unit)
        return pltpu.make_async_remote_copy(
            src_ref=send.at[direction, most],
            dst_ref=recv.at[direction, most],
            send_sem=send_sems.at[direction],
            recv_sem=recv_sems.at[direction],
            device_id=(sec, me),
            device_id_type=MESH,
        )

    names.wait()
    loads[0].wait()
    pack(1)
    pl.semaphore_wait(barrier, peers)
    send_all(1)
    loads[1].wait()
    pack(0)
    send_all(0)

    loads[2].wait()
    slots = peers * cap
    line = lax.broadcasted_iota(jnp.int32, (slots, total), 1)
    slot = lax.broadcasted_iota(jnp.int32, (slots, total), 0)
    expand = (line // unit * cap + lax.rem(line, cap) == slot).astype(bf16)
    for direction in (1, 0):
        wide = tn(hidden[direction], expand).astype(bf16)
        which = lax.rem(lax.broadcasted_iota(jnp.int32, wide.shape, 1) // cap, parts)
        for part in range(parts):
            spread[direction, part] = jnp.where(which == part, wide, jnp.zeros_like(wide))

    own_copy(1).wait()
    all_but_one(1).wait_recv()
    for part in range(parts):
        at = slice(part * chunk, (part + 1) * chunk)
        far_out[:, at] = nn(spread[1, part], recv[1]).astype(bf16)
    exchange = pltpu.make_async_remote_copy(
        src_ref=far_out,
        dst_ref=far_in,
        send_sem=mir_send,
        recv_sem=mir_recv,
        device_id=(mirror, me),
        device_id_type=MESH,
    )
    exchange.start()

    loads[3].wait()
    exchange.wait_recv()
    own_copy(0).wait()
    all_but_one(0).wait_recv()
    saves = []
    for part in range(parts):
        at = slice(part * chunk, (part + 1) * chunk)
        near = nn(spread[0, part], recv[0]).astype(bf16).astype(f32)
        accum[part] = mom[:, at].astype(f32) * momentum_decay + near + far_in[:, at].astype(f32)
        save = pltpu.make_async_copy(accum.at[part], accum_hbm.at[part], out_sems.at[part])
        save.start()
        saves.append(save)
    all_but_one(1).wait_send()
    all_but_one(0).wait_send()
    exchange.wait_send()
    for save in saves:
        save.wait()


def orthogonalize(
    parts, accum_hbm, newm_hbm, upd_hbm, accum, x, gram, newm, upd, in_sems, newm_sems, upd_sems
):
    chunk = accum.shape[2]
    width = parts * chunk
    loads, saves = [], []
    for part in range(parts):
        load = pltpu.make_async_copy(accum_hbm.at[part], accum.at[part], in_sems.at[part])
        load.start()
        loads.append(load)
    squares = None
    for part in range(parts):
        at = slice(part * chunk, (part + 1) * chunk)
        loads[part].wait()
        value = accum[part]
        newm[:, at] = value.astype(bf16)
        save = pltpu.make_async_copy(newm.at[:, at], newm_hbm.at[:, at], newm_sems.at[part])
        save.start()
        saves.append(save)
        square = jnp.sum(value * value, axis=0, keepdims=True)
        squares = square if squares is None else squares + square
    squares = jnp.sum(squares, axis=1, keepdims=True)
    scale = 1.0 / (jnp.sqrt(squares) + norm_epsilon)
    for part in range(parts):
        at = slice(part * chunk, (part + 1) * chunk)
        x[:, at] = (accum[part] * scale).astype(bf16)
    for iteration in range(ITERS):
        gram[...] = nt(x[...], x[...]).astype(bf16)
        for part in range(parts):
            at = slice(part * chunk, (part + 1) * chunk)
            current = x[:, at]
            first = nn(gram[...], current).astype(bf16)
            second = nn(gram[...], first).astype(bf16)
            combined = (
                coef_first * current.astype(f32)
                + coef_second * first.astype(f32)
                + coef_third * second.astype(f32)
            )
            if iteration < ITERS - 1:
                x[:, at] = combined.astype(bf16)
            else:
                upd[:, at] = (combined * math.sqrt(width)).astype(bf16)
                save = pltpu.make_async_copy(upd.at[:, at], upd_hbm.at[:, at], upd_sems.at[part])
                save.start()
                saves.append(save)
    for save in saves:
        save.wait()


def solution(mesh):
    sections, peers = mesh.shape["section"], mesh.shape["expert"]

    def per_device(grad_rows, owner_ids, saved_hidden, momentum):
        _, _, rows, width = grad_rows.shape
        slots, ff = saved_hidden.shape[3:]
        cap = slots // peers
        parts = 16 // cap
        total = slots * parts
        chunk = width // parts
        hbm = pl.BlockSpec(memory_space=pl.ANY)
        accum = pl.pallas_call(
            functools.partial(exchange_rows, sections, peers, cap, parts),
            out_shape=jax.ShapeDtypeStruct((parts, ff, chunk), f32),
            in_specs=[hbm] * 4,
            out_specs=hbm,
            scratch_shapes=[
                pltpu.VMEM((2, rows, width), bf16),
                pltpu.VMEM((2, 1, rows), jnp.int32),
                pltpu.VMEM((2, slots, ff), bf16),
                pltpu.VMEM((ff, width), bf16),
                pltpu.VMEM((2, total, chunk), bf16),
                pltpu.VMEM((2, total, chunk), bf16),
                pltpu.VMEM((2, parts, ff, total), bf16),
                pltpu.VMEM((ff, width), bf16),
                pltpu.VMEM((ff, width), bf16),
                pltpu.VMEM((parts, ff, chunk), f32),
                pltpu.SemaphoreType.DMA((5,)),
                pltpu.SemaphoreType.DMA((2,)),
                pltpu.SemaphoreType.DMA((2,)),
                pltpu.SemaphoreType.DMA((2,)),
                pltpu.SemaphoreType.DMA,
                pltpu.SemaphoreType.DMA,
                pltpu.SemaphoreType.DMA((parts,)),
            ],
            compiler_params=pltpu.CompilerParams(
                collective_id=0, has_side_effects=True, vmem_limit_bytes=VMEM_LIMIT
            ),
            name="routed_rows",
        )(
            grad_rows[0],
            owner_ids.reshape(2, 1, rows),
            saved_hidden.reshape(2, slots, ff),
            momentum[0, 0],
        )
        newm, upd = pl.pallas_call(
            functools.partial(orthogonalize, parts),
            out_shape=[jax.ShapeDtypeStruct((ff, width), bf16)] * 2,
            in_specs=[hbm],
            out_specs=[hbm, hbm],
            scratch_shapes=[
                pltpu.VMEM((parts, ff, chunk), f32),
                pltpu.VMEM((ff, width), bf16),
                pltpu.VMEM((ff, ff), bf16),
                pltpu.VMEM((ff, width), bf16),
                pltpu.VMEM((ff, width), bf16),
                pltpu.SemaphoreType.DMA((parts,)),
                pltpu.SemaphoreType.DMA((parts,)),
                pltpu.SemaphoreType.DMA((parts,)),
            ],
            compiler_params=pltpu.CompilerParams(vmem_limit_bytes=VMEM_LIMIT),
            name="orthogonalize",
        )(accum)
        return newm[None, None], upd[None, None]

    placed = (
        P("section", None, "expert", None),
        P("section", None, "expert", None),
        P("section", None, "expert", None, None),
        P("section", "expert", None, None),
    )
    return jax.shard_map(
        per_device,
        mesh=mesh,
        in_specs=placed,
        out_specs=(P("section", "expert", None, None), P("section", "expert", None, None)),
        check_vma=False,
    )
```
